32 devices in a mesh: row: 8 (over z, core), col: 4 (over y, x).
Axes of the slice: x: 2, y: 2, z: 4, core: 2. Of those that a mesh axis runs over, the one named last changes fastest.
Arguments:
- weights: bfloat16 [2, 24576, 6144], P(None, 'row', 'col'), may hold values from -0.109375 to 0.109375
- pattern: int32 [2, 192, 48], P(None, 'row', 'col'), may hold values 0 or 1
- sketch: bfloat16 [6144, 512], P('col'), may hold values from -6 to 6
Outputs:
- basis: float32 [2, 24576, 512], P(None, ('row', 'col'))
The draws below stay inside these ranges and needn't reach their ends.
Inputs may be any that keep to these rules, and one draw needn't show every extreme that they name: `pattern`: 1 marks a block of the sparse part, 0 a block of the residual.
All inputs are finite; a program needn't handle non-finite values.
Results may differ from the reference program's by a relative error of at most 0.0003.
Values sent between devices are 32-bit elements; how exact they have to be, the bound alone decides.
A program may use at most 128 MiB of HBM per device.

```python
import jax
import jax.numpy as jnp
from jax import lax

M = 24576
N = 6144
K = 512
BLOCK = 128
LAYERS = 2
ROW_BLOCKS = 192
COL_BLOCKS = 48


def set_ends(array, stream_key, least, top_value):
    longest = array.shape.index(max(array.shape))
    spots = []
    for shift in (0, 1):
        where = [jax.random.randint(jax.random.fold_in(stream_key, axis), (), 0, length) for axis, length in enumerate(array.shape)]
        where[longest] = (where[longest] + shift) % array.shape[longest]
        spots.append(tuple(where))
    return array.at[spots[0]].set(least).at[spots[1]].set(top_value)


def with_spikes(entries, rng, source, target, shards_of, factor):
    def block_of(dim):
        return (jnp.arange(entries.shape[dim]) // (entries.shape[dim] // shards_of)).reshape((-1,) + (1,) * (entries.ndim - 1 - dim))

    first = jax.random.permutation(rng, shards_of)[block_of(target)]
    far = (block_of(target) + shards_of // 2) % shards_of
    return jnp.where((block_of(source) == first) | (block_of(source) == far), factor * entries, entries)


def block_levels(stream_key, dims, cuts, least, largest):
    def one(position, shards_of):
        heights = jax.random.uniform(jax.random.fold_in(jax.random.fold_in(stream_key, 6), position), (shards_of,), jnp.float32, least / len(cuts), largest / len(cuts))
        return jnp.repeat(jnp.exp(heights), dims[position] // shards_of).reshape((-1,) + (1,) * (len(dims) - position - 1))

    factor_of = one(*cuts[0])
    for cut in cuts[1:]:
        factor_of = factor_of * one(*cut)
    return factor_of


def normal_values(own_key, shape, width, limit, cuts=(), kind=jnp.bfloat16):
    drawn = width * jax.random.normal(own_key, shape, jnp.float32)
    if cuts:
        drawn = drawn * block_levels(own_key, shape, cuts, -0.22, 0.18)
    return jnp.clip(drawn, -limit, limit).astype(kind)


def gaussian_with(key, extent, spread, most, split, heavy, kind=jnp.bfloat16):
    result = spread * jax.random.normal(key, extent, jnp.float32)
    if split:
        result = result * block_levels(key, extent, split, -0.22, 0.18)
    return jnp.clip(with_spikes(result, jax.random.fold_in(key, 3), *heavy), -most, most).astype(kind)


def setup_inputs(seed: int = 0) -> dict:
    splits = jax.random.split(jax.random.key(seed), 4)
    return {
        "weights": gaussian_with(splits[0], (LAYERS, M, N), N ** -0.5, 0.109375, ((1, 8), (2, 4)), (2, 1, 8, 2.0)),
        "pattern": set_ends((jax.random.randint(splits[1], (LAYERS, ROW_BLOCKS, COL_BLOCKS), 0, 2) < 1).astype(jnp.int32), jax.random.fold_in(splits[1], 1), 0, 1),
        "sketch": normal_values(splits[2], (N, K), 1.0, 6.0, ((0, 4),)),
    }


def one_layer(weight, marks, sketch):
    keep = (1 - marks).astype(weight.dtype)
    shaped = weight.reshape(ROW_BLOCKS, BLOCK, COL_BLOCKS, BLOCK) * keep[:, None, :, None]
    leftover = shaped.reshape(M, N)
    sampled = jnp.dot(leftover.astype(jnp.float32), sketch.astype(jnp.float32), preferred_element_type=jnp.float32)
    gram = lax.dot_general(sampled.astype(jnp.float32), sampled.astype(jnp.float32), (((0,), (0,)), ((), ())), precision=lax.Precision.HIGHEST, preferred_element_type=jnp.float32) / M
    lower = jnp.linalg.cholesky(gram)
    solved = lax.linalg.triangular_solve(lower, sampled, left_side=False, lower=True, transpose_a=True)
    return solved * jnp.sqrt(jnp.float32(M))

def reference(weights, pattern, sketch):
    outputs = [one_layer(weights[layer], pattern[layer], sketch) for layer in range(LAYERS)]
    return jnp.stack(outputs, axis=0)
```

```python
import jax
import jax.numpy as jnp
from jax import lax
from jax.experimental import pallas as pl
from jax.experimental.pallas import tpu as pltpu
from jax.sharding import PartitionSpec as P

BLOCK = 128
LAYERS = 2
GROUP = 8


def split(x):
    high = x.astype(jnp.bfloat16)
    low = (x - high.astype(jnp.float32)).astype(jnp.bfloat16)
    return high, low


def dot3(a, b, dims):
    a_high, a_low = split(a)
    b_high, b_low = split(b)

    def one(x, y):
        return lax.dot_general(x, y, (dims, ((), ())), preferred_element_type=jnp.float32)

    return one(a_high, b_high) + (one(a_high, b_low) + one(a_low, b_high))


def sample_kernel(keep_ref, w_ref, s_ref, o_ref):
    rows = w_ref.shape[1]
    parts = []
    for block in range(rows // BLOCK):
        parts.append(w_ref[0, block * BLOCK : (block + 1) * BLOCK, :] * keep_ref[0, block])
    leftover = jnp.concatenate(parts, axis=0)
    o_ref[...] = jnp.dot(leftover, s_ref[...], preferred_element_type=jnp.float32)


def sample(weights, keep, sketch, layer):
    _, row_count, col_count = weights.shape
    width = sketch.shape[1]
    tile = min(512, row_count)
    while row_count % tile:
        tile -= BLOCK
    return pl.pallas_call(
        sample_kernel,
        grid=(row_count // tile,),
        in_specs=[
            pl.BlockSpec((1, tile // BLOCK, 1, col_count), lambda i: (layer, i, 0, 0)),
            pl.BlockSpec((1, tile, col_count), lambda i: (layer, i, 0)),
            pl.BlockSpec((col_count, width), lambda i: (0, 0)),
        ],
        out_specs=pl.BlockSpec((tile, width), lambda i: (i, 0)),
        out_shape=jax.ShapeDtypeStruct((row_count, width), jnp.float32),
        compiler_params=pltpu.CompilerParams(vmem_limit_bytes=40 * 2**20),
        cost_estimate=pl.CostEstimate(
            flops=2 * row_count * col_count * width,
            bytes_accessed=2 * row_count * col_count + 4 * row_count * width,
            transcendentals=0,
        ),
        name="sample",
    )(keep, weights, sketch)


def factor_block(d, size):
    row = lax.broadcasted_iota(jnp.int32, (size, size), 0)
    col = lax.broadcasted_iota(jnp.int32, (size, size), 1)
    e = (row == col).astype(jnp.float32)
    sub = lax.broadcasted_iota(jnp.int32, (GROUP, size), 0)
    done = []
    for start in range(0, size, GROUP):
        live = size - start
        cols = [
            jnp.broadcast_to(d[:, start + k : start + k + 1], (live, size)) for k in range(GROUP)
        ]
        head_cols = [c[:GROUP] for c in cols]
        tail_cols = [c[GROUP:] for c in cols]
        head_d, tail_d = d[:GROUP], d[GROUP:]
        head_e, tail_e = e[:GROUP], e[GROUP:]
        scale = jnp.zeros((GROUP, size), jnp.float32)
        for k in range(GROUP):
            pivot = head_cols[k][k : k + 1]
            inverse = 1.0 / pivot
            scale = jnp.where(sub == k, lax.rsqrt(pivot), scale)
            factor = jnp.where(sub > k, head_cols[k], 0.0)
            row_e = head_e[k : k + 1] * inverse
            row_d = head_d[k : k + 1] * inverse
            for j in range(k + 1, GROUP):
                step = head_cols[j][k : k + 1] * inverse
                head_cols[j] = head_cols[j] - factor * step
                if live > GROUP:
                    tail_cols[j] = tail_cols[j] - tail_cols[k] * step
            head_d = head_d - factor * row_d
            head_e = head_e - factor * row_e
            if live > GROUP:
                tail_d = tail_d - tail_cols[k] * row_d
                tail_e = tail_e - tail_cols[k] * row_e
        done.append(head_e * scale)
        d, e = tail_d, tail_e
    return jnp.concatenate(done, axis=0)


def inverse_kernel(total_rows, g_ref, o_ref, a, x):
    width = g_ref.shape[0]
    count = width // BLOCK
    a[...] = g_ref[...]
    x[...] = jnp.zeros_like(x)

    @pl.loop(0, count)
    def _(k):
        here = pl.ds(pl.multiple_of(k * BLOCK, BLOCK), BLOCK)
        inner = factor_block(a[here, here], BLOCK)
        for now in range(count):

            @pl.when(k == now)
            def _():
                lo, hi = now * BLOCK, (now + 1) * BLOCK
                if now:
                    mine = dot3(inner, x[lo:hi, :lo], ((1,), (0,)))
                    x[lo:hi, :lo] = mine
                x[lo:hi, lo:hi] = inner
                if now < count - 1:
                    right = dot3(inner, a[lo:hi, hi:], ((1,), (0,)))
                    a[hi:, hi:] -= dot3(right, right, ((0,), (0,)))
                    x[hi:, :hi] -= dot3(right, x[lo:hi, :hi], ((0,), (0,)))

    o_ref[...] = x[...].T * jnp.float32(total_rows)


def invert(g, total_rows):
    width = g.shape[0]
    return pl.pallas_call(
        lambda *refs: inverse_kernel(total_rows, *refs),
        in_specs=[pl.BlockSpec(memory_space=pltpu.VMEM)],
        out_specs=pl.BlockSpec(memory_space=pltpu.VMEM),
        out_shape=jax.ShapeDtypeStruct((width, width), jnp.float32),
        scratch_shapes=[pltpu.VMEM((width, width), jnp.float32)] * 2,
        compiler_params=pltpu.CompilerParams(vmem_limit_bytes=40 * 2**20),
        cost_estimate=pl.CostEstimate(
            flops=40 * 10**9, bytes_accessed=8 * width * width, transcendentals=0
        ),
        name="invert",
    )(g)


def apply_kernel(r_ref, u_ref, *rest):
    rest[-1][0] = dot3(r_ref[...], u_ref[...], ((1,), (0,)))


def apply(rows_here, upper, layer, out):
    row_count, width = rows_here.shape
    tile = min(256, row_count)
    while row_count % tile:
        tile -= 8
    extra = [] if out is None else [pl.BlockSpec(memory_space=pl.ANY)]
    return pl.pallas_call(
        apply_kernel,
        grid=(row_count // tile,),
        in_specs=[
            pl.BlockSpec((tile, width), lambda i: (i, 0)),
            pl.BlockSpec((width, width), lambda i: (0, 0)),
        ]
        + extra,
        out_specs=pl.BlockSpec((1, tile, width), lambda i: (layer, i, 0)),
        out_shape=jax.ShapeDtypeStruct((LAYERS, row_count, width), jnp.float32),
        input_output_aliases={} if out is None else {2: 0},
        compiler_params=pltpu.CompilerParams(vmem_limit_bytes=40 * 2**20),
        cost_estimate=pl.CostEstimate(
            flops=6 * row_count * width * width,
            bytes_accessed=8 * row_count * width,
            transcendentals=0,
        ),
        name="apply",
    )(rows_here, upper, *([] if out is None else [out]))


def local_gram(rows_here):
    return lax.dot_general(
        rows_here,
        rows_here,
        (((0,), (0,)), ((), ())),
        precision=lax.Precision.HIGH,
        preferred_element_type=jnp.float32,
    )


def make_body(total_shards):
    def body(weights, pattern, sketch):
        total_rows = weights.shape[1] * total_shards
        keep = jnp.repeat((1 - pattern).astype(jnp.bfloat16), BLOCK, axis=2)[:, :, None, :]
        rows = []
        for layer in range(LAYERS):
            part = sample(weights, keep, sketch, layer)
            rows.append(lax.psum_scatter(part, "col", scatter_dimension=0, tiled=True))
        out = None
        for layer in range(LAYERS):
            gram = lax.psum(local_gram(rows[layer]), ("row", "col"))
            out = apply(rows[layer], invert(gram, total_rows), layer, out)
        return out

    return body


def solution(mesh):
    return jax.shard_map(
        make_body(mesh.shape["row"]),
        mesh=mesh,
        in_specs=(P(None, "row", "col"), P(None, "row", "col"), P("col", None)),
        out_specs=P(None, ("row", "col"), None),
        check_vma=False,
    )
```

```python
import jax
import jax.numpy as jnp
from jax import lax
from jax.experimental import pallas as pl
from jax.experimental.pallas import tpu as pltpu
from jax.sharding import PartitionSpec as P

BLOCK = 128
LAYERS = 2
GROUP = 8


def split(x):
    high = x.astype(jnp.bfloat16)
    low = (x - high.astype(jnp.float32)).astype(jnp.bfloat16)
    return high, low


def dot3(a, b, dims):
    a_high, a_low = split(a)
    b_high, b_low = split(b)

    def one(x, y):
        return lax.dot_general(x, y, (dims, ((), ())), preferred_element_type=jnp.float32)

    return one(a_high, b_high) + (one(a_high, b_low) + one(a_low, b_high))


def sample_kernel(keep_ref, w_ref, s_ref, o_ref):
    rows = w_ref.shape[1]
    parts = []
    for block in range(rows // BLOCK):
        parts.append(w_ref[0, block * BLOCK : (block + 1) * BLOCK, :] * keep_ref[0, block])
    leftover = jnp.concatenate(parts, axis=0)
    o_ref[...] = jnp.dot(leftover, s_ref[...], preferred_element_type=jnp.float32)


def sample(weights, keep, sketch, layer):
    _, row_count, col_count = weights.shape
    width = sketch.shape[1]
    tile = min(512, row_count)
    while row_count % tile:
        tile -= BLOCK
    return pl.pallas_call(
        sample_kernel,
        grid=(row_count // tile,),
        in_specs=[
            pl.BlockSpec((1, tile // BLOCK, 1, col_count), lambda i: (layer, i, 0, 0)),
            pl.BlockSpec((1, tile, col_count), lambda i: (layer, i, 0)),
            pl.BlockSpec((col_count, width), lambda i: (0, 0)),
        ],
        out_specs=pl.BlockSpec((tile, width), lambda i: (i, 0)),
        out_shape=jax.ShapeDtypeStruct((row_count, width), jnp.float32),
        compiler_params=pltpu.CompilerParams(vmem_limit_bytes=40 * 2**20),
        cost_estimate=pl.CostEstimate(
            flops=2 * row_count * col_count * width,
            bytes_accessed=2 * row_count * col_count + 4 * row_count * width,
            transcendentals=0,
        ),
        name="sample",
    )(keep, weights, sketch)


def factor_blocks(blocks, size):
    many = range(len(blocks))
    row = lax.broadcasted_iota(jnp.int32, (size, size), 0)
    col = lax.broadcasted_iota(jnp.int32, (size, size), 1)
    eye = (row == col).astype(jnp.float32)
    sub = lax.broadcasted_iota(jnp.int32, (GROUP, size), 0)
    d = list(blocks)
    e = [eye for _ in many]
    done = [[] for _ in many]
    for start in range(0, size, GROUP):
        live = size - start
        cols = [
            [
                jnp.broadcast_to(d[n][:, start + k : start + k + 1], (live, size))
                for k in range(GROUP)
            ]
            for n in many
        ]
        head_cols = [[c[:GROUP] for c in cols[n]] for n in many]
        tail_cols = [[c[GROUP:] for c in cols[n]] for n in many]
        head_d, tail_d = [x[:GROUP] for x in d], [x[GROUP:] for x in d]
        head_e, tail_e = [x[:GROUP] for x in e], [x[GROUP:] for x in e]
        scale = [jnp.zeros((GROUP, size), jnp.float32) for _ in many]
        for k in range(GROUP):
            for n in many:
                pivot = head_cols[n][k][k : k + 1]
                inverse = 1.0 / pivot
                scale[n] = jnp.where(sub == k, lax.rsqrt(pivot), scale[n])
                factor = jnp.where(sub > k, head_cols[n][k], 0.0)
                row_e = head_e[n][k : k + 1] * inverse
                row_d = head_d[n][k : k + 1] * inverse
                for j in range(k + 1, GROUP):
                    step = head_cols[n][j][k : k + 1] * inverse
                    head_cols[n][j] = head_cols[n][j] - factor * step
                    if live > GROUP:
                        tail_cols[n][j] = tail_cols[n][j] - tail_cols[n][k] * step
                head_d[n] = head_d[n] - factor * row_d
                head_e[n] = head_e[n] - factor * row_e
                if live > GROUP:
                    tail_d[n] = tail_d[n] - tail_cols[n][k] * row_d
                    tail_e[n] = tail_e[n] - tail_cols[n][k] * row_e
        for n in many:
            done[n].append(head_e[n] * scale[n])
        d, e = tail_d, tail_e
    return [jnp.concatenate(done[n], axis=0) for n in many]


def upper_blocks(width):
    count = width // BLOCK
    return [(i, j) for i in range(count) for j in range(i, count)]


def inverse_kernel(total_rows, g_ref, o_ref, a, x):
    layers, width = a.shape[0], a.shape[1]
    count = width // BLOCK
    a[...] = jnp.zeros_like(a)
    x[...] = jnp.zeros_like(x)
    for b, (i, j) in enumerate(upper_blocks(width)):
        for n in range(layers):
            a[n, i * BLOCK : (i + 1) * BLOCK, j * BLOCK : (j + 1) * BLOCK] = g_ref[
                n, b * BLOCK : (b + 1) * BLOCK
            ]

    @pl.loop(0, count)
    def _(k):
        here = pl.ds(pl.multiple_of(k * BLOCK, BLOCK), BLOCK)
        inners = factor_blocks([a[n, here, here] for n in range(layers)], BLOCK)
        for now in range(count):

            @pl.when(k == now)
            def _():
                lo, hi = now * BLOCK, (now + 1) * BLOCK
                for n in range(layers):
                    if now:
                        x[n, lo:hi, :lo] = dot3(inners[n], x[n, lo:hi, :lo], ((1,), (0,)))
                    x[n, lo:hi, lo:hi] = inners[n]
                    if now < count - 1:
                        right = dot3(inners[n], a[n, lo:hi, hi:], ((1,), (0,)))
                        a[n, hi:, hi:] -= dot3(right, right, ((0,), (0,)))
                        x[n, hi:, :hi] -= dot3(right, x[n, lo:hi, :hi], ((0,), (0,)))

    for n in range(layers):
        o_ref[n] = x[n].T * jnp.float32(total_rows)


def invert(g, width, total_rows):
    layers = g.shape[0]
    return pl.pallas_call(
        lambda *refs: inverse_kernel(total_rows, *refs),
        in_specs=[pl.BlockSpec(memory_space=pltpu.VMEM)],
        out_specs=pl.BlockSpec(memory_space=pltpu.VMEM),
        out_shape=jax.ShapeDtypeStruct((layers, width, width), jnp.float32),
        scratch_shapes=[pltpu.VMEM((layers, width, width), jnp.float32)] * 2,
        compiler_params=pltpu.CompilerParams(vmem_limit_bytes=40 * 2**20),
        cost_estimate=pl.CostEstimate(
            flops=40 * 10**9, bytes_accessed=8 * width * width, transcendentals=0
        ),
        name="invert",
    )(g)


def apply_kernel(r_ref, u_ref, o_ref):
    o_ref[0] = dot3(r_ref[0], u_ref[0], ((1,), (0,)))


def apply(rows_here, upper):
    layers, row_count, width = rows_here.shape
    tile = min(256, row_count)
    while row_count % tile:
        tile -= 8
    return pl.pallas_call(
        apply_kernel,
        grid=(layers, row_count // tile),
        in_specs=[
            pl.BlockSpec((1, tile, width), lambda l, i: (l, i, 0)),
            pl.BlockSpec((1, width, width), lambda l, i: (l, 0, 0)),
        ],
        out_specs=pl.BlockSpec((1, tile, width), lambda l, i: (l, i, 0)),
        out_shape=jax.ShapeDtypeStruct((layers, row_count, width), jnp.float32),
        compiler_params=pltpu.CompilerParams(vmem_limit_bytes=40 * 2**20),
        cost_estimate=pl.CostEstimate(
            flops=6 * layers * row_count * width * width,
            bytes_accessed=8 * layers * row_count * width,
            transcendentals=0,
        ),
        name="apply",
    )(rows_here, upper)


MESH = pl.DeviceIdType.MESH


def remote(src, dst, send, recv, device):
    return pltpu.make_async_remote_copy(
        src_ref=src, dst_ref=dst, send_sem=send, recv_sem=recv, device_id=device, device_id_type=MESH
    )


def fused_kernel(
    cols, chips, keep_ref, w_ref, s_ref, rows_ref, g_ref,
    wbuf, part, inbox, pack, pair, box, full,
    wsem, rs_send, rs_recv, pair_send, pair_recv, out_send, out_recv, all_send, all_recv,
    back_send, back_recv,
):
    row, col = lax.axis_index("row"), lax.axis_index("col")
    core, z = row % 2, row // 2
    cx, cy = col % 2, col // 2
    me = z * cols + col
    half = wbuf.shape[1]
    width = s_ref.shape[1]
    blocks = half // BLOCK
    share = pack.shape[1] // 2
    piece = share // chips
    to_x = (row, cy * 2 + (1 - cx))
    to_y = (row, (1 - cy) * 2 + cx)
    partner = (row + 1 - 2 * core, col)

    def peer(offset):
        p = (me + offset) % chips
        return p, ((p // cols) * 2 + core, p % cols)

    barrier = pltpu.get_barrier_semaphore()
    pl.semaphore_signal(barrier, inc=1, device_id=partner, device_id_type=MESH)
    for offset in range(1, chips):
        pl.semaphore_signal(barrier, inc=1, device_id=peer(offset)[1], device_id_type=MESH)

    slots = [(1, 1, 0), (1, 1, 1), (1, 0, 0), (0, 1, 1), (0, 1, 0), (1, 0, 1), (0, 0, 0), (0, 0, 1)]

    def first_block(slot):
        dx, dy, part_of = slots[slot]
        owner = ((cy + dy) % 2) * 2 + (cx + dx) % 2
        return (owner * 2 + part_of) * blocks

    def fetch(step):
        layer, slot = step // 8, step % 8
        start = pl.multiple_of(first_block(slot) * BLOCK, BLOCK)
        return pltpu.make_async_copy(
            w_ref.at[layer, pl.ds(start, half)], wbuf.at[step % 2], wsem.at[step % 2]
        )

    def product(step):
        layer, slot = step // 8, step % 8
        if step + 1 < 8 * LAYERS:
            fetch(step + 1).start()
        fetch(step).wait()
        first = first_block(slot)
        kept = [
            wbuf[step % 2, b * BLOCK : (b + 1) * BLOCK, :] * keep_ref[layer, first + b]
            for b in range(blocks)
        ]
        part[layer, slot] = jnp.dot(
            jnp.concatenate(kept, axis=0), s_ref[...], preferred_element_type=jnp.float32
        )

    targets = [to_x, to_y, to_x, to_y, to_y, to_x]

    def hop(layer, k):
        return remote(
            part.at[layer, k], inbox.at[layer, k],
            rs_send.at[layer, k], rs_recv.at[layer, k], targets[k],
        )

    def combine(layer):
        for k in (0, 1):
            hop(layer, k).wait_recv()
            part[layer, 4 + k] += inbox[layer, k]
            hop(layer, 4 + k).start()

    def gather_rows(layer):
        for k in (0, 1):
            hop(layer, 2 + k).wait_recv()
            hop(layer, 4 + k).wait_recv()
            rows_ref[layer, k * half : (k + 1) * half] = (
                part[layer, 6 + k] + inbox[layer, 2 + k] + inbox[layer, 4 + k]
            )

    def gram(layer):
        at = 0
        for i in range(width // BLOCK):
            lo = i * BLOCK
            g = dot3(
                rows_ref[layer, :, lo : lo + BLOCK], rows_ref[layer, :, lo:], ((0,), (0,))
            )
            for j in range((width - lo) // BLOCK):
                pack[layer, at : at + BLOCK] = g[:, j * BLOCK : (j + 1) * BLOCK]
                at += BLOCK

    def pair_copy(layer):
        other = pl.ds(pl.multiple_of((1 - core) * share, 8), share)
        return remote(
            pack.at[layer, other], pair.at[layer],
            pair_send.at[layer], pair_recv.at[layer], partner,
        )

    def out_copy(layer, offset):
        p, device = peer(offset)
        mine = pl.ds(pl.multiple_of(core * share + p * piece, 8), piece)
        return remote(
            pack.at[layer, mine], box.at[layer, offset],
            out_send.at[layer, offset], out_recv.at[layer, offset], device,
        )

    def all_copy(layer, offset):
        device = peer(offset)[1]
        here = full.at[layer, core, pl.ds(pl.multiple_of(me * piece, 8), piece)]
        return remote(
            here, here, all_send.at[layer, offset], all_recv.at[layer, offset], device
        )

    def back_copy(layer):
        here = full.at[layer, core]
        return remote(here, here, back_send.at[layer], back_recv.at[layer], partner)

    def sum_start(layer):
        pair_copy(layer).start()
        pair_copy(layer).wait_recv()
        own = pl.ds(pl.multiple_of(core * share, 8), share)
        pack[layer, own] += pair[layer]
        for offset in range(1, chips):
            out_copy(layer, offset).start()

    def sum_middle(layer):
        mine = pl.ds(pl.multiple_of(core * share + me * piece, 8), piece)
        total = pack[layer, mine]
        for offset in range(1, chips):
            out_copy(layer, offset).wait_recv()
            total = total + box[layer, offset]
        full[layer, core, pl.ds(pl.multiple_of(me * piece, 8), piece)] = total
        for offset in range(1, chips):
            all_copy(layer, offset).start()

    def sum_end(layer):
        for offset in range(1, chips):
            all_copy(layer, offset).wait_recv()
        back_copy(layer).start()
        back_copy(layer).wait_recv()
        for c in range(2):
            g_ref[layer, c * share : (c + 1) * share] = full[layer, c]

    fetch(0).start()
    for slot in range(8):
        product(slot)
        if slot == 0:
            pl.semaphore_wait(barrier, chips)
        if slot < 4:
            hop(0, slot).start()
    for slot in range(4):
        product(8 + slot)
    combine(0)
    for slot in range(4):
        hop(1, slot).start()
    for slot in range(4, 8):
        product(8 + slot)
    gather_rows(0)
    gram(0)
    sum_start(0)
    combine(1)
    sum_middle(0)
    sum_end(0)
    gather_rows(1)
    gram(1)
    sum_start(1)
    sum_middle(1)
    sum_end(1)

    for layer in range(LAYERS):
        for k in range(6):
            hop(layer, k).wait_send()
        pair_copy(layer).wait_send()
        back_copy(layer).wait_send()
        for offset in range(1, chips):
            out_copy(layer, offset).wait_send()
            all_copy(layer, offset).wait_send()


def fused(weights, keep, sketch, cols, chips):
    _, row_count, col_count = weights.shape
    width = sketch.shape[1]
    rows_here = row_count // cols
    half = rows_here // 2
    packed = len(upper_blocks(width)) * BLOCK
    share = packed // 2
    vmem = pl.BlockSpec(memory_space=pltpu.VMEM)
    f32 = jnp.float32
    dma = pltpu.SemaphoreType.DMA
    return pl.pallas_call(
        lambda *refs: fused_kernel(cols, chips, *refs),
        in_specs=[vmem, pl.BlockSpec(memory_space=pl.ANY), vmem],
        out_specs=[vmem, vmem],
        out_shape=[
            jax.ShapeDtypeStruct((LAYERS, rows_here, width), f32),
            jax.ShapeDtypeStruct((LAYERS, packed, BLOCK), f32),
        ],
        scratch_shapes=[
            pltpu.VMEM((2, half, col_count), jnp.bfloat16),
            pltpu.VMEM((LAYERS, 8, half, width), f32),
            pltpu.VMEM((LAYERS, 6, half, width), f32),
            pltpu.VMEM((LAYERS, packed, BLOCK), f32),
            pltpu.VMEM((LAYERS, share, BLOCK), f32),
            pltpu.VMEM((LAYERS, chips, share // chips, BLOCK), f32),
            pltpu.VMEM((LAYERS, 2, share, BLOCK), f32),
            dma((2,)),
            dma((LAYERS, 6)),
            dma((LAYERS, 6)),
            dma((LAYERS,)),
            dma((LAYERS,)),
            dma((LAYERS, chips)),
            dma((LAYERS, chips)),
            dma((LAYERS, chips)),
            dma((LAYERS, chips)),
            dma((LAYERS,)),
            dma((LAYERS,)),
        ],
        compiler_params=pltpu.CompilerParams(
            vmem_limit_bytes=56 * 2**20, collective_id=0, has_side_effects=True
        ),
        cost_estimate=pl.CostEstimate(
            flops=2 * LAYERS * row_count * col_count * width,
            bytes_accessed=2 * LAYERS * row_count * col_count,
            transcendentals=0,
        ),
        name="fused",
    )(keep, weights, sketch)


def local_gram(rows_here):
    return lax.dot_general(
        rows_here,
        rows_here,
        (((0,), (0,)), ((), ())),
        precision=lax.Precision.HIGH,
        preferred_element_type=jnp.float32,
    )


def make_body(mesh):
    rows, cols = mesh.shape["row"], mesh.shape["col"]
    chips = rows // 2 * cols

    def body(weights, pattern, sketch):
        total_rows = weights.shape[1] * rows
        width = sketch.shape[1]
        blocks = upper_blocks(width)
        keep = jnp.repeat((1 - pattern).astype(jnp.bfloat16), BLOCK, axis=2)[:, :, None, :]
        if cols == 4 and rows % 2 == 0 and (len(blocks) * BLOCK) % (2 * chips * 8) == 0:
            sampled, gram = fused(weights, keep, sketch, cols, chips)
        else:
            sampled = jnp.stack(
                [
                    lax.psum_scatter(
                        sample(weights, keep, sketch, layer), "col", scatter_dimension=0, tiled=True
                    )
                    for layer in range(LAYERS)
                ]
            )
            g = [local_gram(sampled[layer]) for layer in range(LAYERS)]
            packed = jnp.stack(
                [
                    jnp.concatenate(
                        [
                            x[i * BLOCK : (i + 1) * BLOCK, j * BLOCK : (j + 1) * BLOCK]
                            for i, j in blocks
                        ]
                    )
                    for x in g
                ]
            )
            gram = lax.psum(packed, ("row", "col"))
        return apply(sampled, invert(gram, width, total_rows))

    return body


def solution(mesh):
    return jax.shard_map(
        make_body(mesh),
        mesh=mesh,
        in_specs=(P(None, "row", "col"), P(None, "row", "col"), P("col", None)),
        out_specs=P(None, ("row", "col"), None),
        check_vma=False,
    )
```

```python
import jax
import jax.numpy as jnp
from jax import lax
from jax.experimental import pallas as pl
from jax.experimental.pallas import tpu as pltpu
from jax.sharding import PartitionSpec as P

BLOCK = 128
LAYERS = 2
GROUP = 8


def split(x):
    high = x.astype(jnp.bfloat16)
    low = (x - high.astype(jnp.float32)).astype(jnp.bfloat16)
    return high, low


def dot3(a, b, dims):
    a_high, a_low = split(a)
    b_high, b_low = split(b)

    def one(x, y):
        return lax.dot_general(x, y, (dims, ((), ())), preferred_element_type=jnp.float32)

    return one(a_high, b_high) + (one(a_high, b_low) + one(a_low, b_high))


def sample_kernel(keep_ref, w_ref, s_ref, o_ref):
    rows = w_ref.shape[1]
    parts = []
    for block in range(rows // BLOCK):
        parts.append(w_ref[0, block * BLOCK : (block + 1) * BLOCK, :] * keep_ref[0, block])
    leftover = jnp.concatenate(parts, axis=0)
    o_ref[...] = jnp.dot(leftover, s_ref[...], preferred_element_type=jnp.float32)


def sample(weights, keep, sketch, layer):
    _, row_count, col_count = weights.shape
    width = sketch.shape[1]
    tile = min(512, row_count)
    while row_count % tile:
        tile -= BLOCK
    return pl.pallas_call(
        sample_kernel,
        grid=(row_count // tile,),
        in_specs=[
            pl.BlockSpec((1, tile // BLOCK, 1, col_count), lambda i: (layer, i, 0, 0)),
            pl.BlockSpec((1, tile, col_count), lambda i: (layer, i, 0)),
            pl.BlockSpec((col_count, width), lambda i: (0, 0)),
        ],
        out_specs=pl.BlockSpec((tile, width), lambda i: (i, 0)),
        out_shape=jax.ShapeDtypeStruct((row_count, width), jnp.float32),
        compiler_params=pltpu.CompilerParams(vmem_limit_bytes=40 * 2**20),
        cost_estimate=pl.CostEstimate(
            flops=2 * row_count * col_count * width,
            bytes_accessed=2 * row_count * col_count + 4 * row_count * width,
            transcendentals=0,
        ),
        name="sample",
    )(keep, weights, sketch)


def factor_blocks(blocks, size):
    many = range(len(blocks))
    row = lax.broadcasted_iota(jnp.int32, (size, size), 0)
    col = lax.broadcasted_iota(jnp.int32, (size, size), 1)
    eye = (row == col).astype(jnp.float32)
    sub = lax.broadcasted_iota(jnp.int32, (GROUP, size), 0)
    d = list(blocks)
    e = [eye for _ in many]
    done = [[] for _ in many]
    for start in range(0, size, GROUP):
        live = size - start
        cols = [
            [
                jnp.broadcast_to(d[n][:, start + k : start + k + 1], (live, size))
                for k in range(GROUP)
            ]
            for n in many
        ]
        head_cols = [[c[:GROUP] for c in cols[n]] for n in many]
        tail_cols = [[c[GROUP:] for c in cols[n]] for n in many]
        head_d, tail_d = [x[:GROUP] for x in d], [x[GROUP:] for x in d]
        head_e, tail_e = [x[:GROUP] for x in e], [x[GROUP:] for x in e]
        scale = [jnp.zeros((GROUP, size), jnp.float32) for _ in many]
        for k in range(GROUP):
            for n in many:
                pivot = head_cols[n][k][k : k + 1]
                inverse = 1.0 / pivot
                scale[n] = jnp.where(sub == k, lax.rsqrt(pivot), scale[n])
                factor = jnp.where(sub > k, head_cols[n][k], 0.0)
                row_e = head_e[n][k : k + 1] * inverse
                row_d = head_d[n][k : k + 1] * inverse
                for j in range(k + 1, GROUP):
                    step = head_cols[n][j][k : k + 1] * inverse
                    head_cols[n][j] = head_cols[n][j] - factor * step
                    if live > GROUP:
                        tail_cols[n][j] = tail_cols[n][j] - tail_cols[n][k] * step
                head_d[n] = head_d[n] - factor * row_d
                head_e[n] = head_e[n] - factor * row_e
                if live > GROUP:
                    tail_d[n] = tail_d[n] - tail_cols[n][k] * row_d
                    tail_e[n] = tail_e[n] - tail_cols[n][k] * row_e
        for n in many:
            done[n].append(head_e[n] * scale[n])
        d, e = tail_d, tail_e
    return [jnp.concatenate(done[n], axis=0) for n in many]


def upper_blocks(width):
    count = width // BLOCK
    return [(i, j) for i in range(count) for j in range(i, count)]


def inverse_of(total_rows, g_ref, o_ref, a, x, many):
    width = a.shape[1]
    count = width // BLOCK
    for n in many:
        a[n] = jnp.zeros((width, width), jnp.float32)
        x[n] = jnp.zeros((width, width), jnp.float32)
        for b, (i, j) in enumerate(upper_blocks(width)):
            a[n, i * BLOCK : (i + 1) * BLOCK, j * BLOCK : (j + 1) * BLOCK] = g_ref[
                n, b * BLOCK : (b + 1) * BLOCK
            ]

    @pl.loop(0, count)
    def _(k):
        here = pl.ds(pl.multiple_of(k * BLOCK, BLOCK), BLOCK)
        inners = factor_blocks([a[n, here, here] for n in many], BLOCK)
        for now in range(count):

            @pl.when(k == now)
            def _():
                lo, hi = now * BLOCK, (now + 1) * BLOCK
                for n, inner in zip(many, inners):
                    if now:
                        x[n, lo:hi, :lo] = dot3(inner, x[n, lo:hi, :lo], ((1,), (0,)))
                    x[n, lo:hi, lo:hi] = inner
                    if now < count - 1:
                        right = dot3(inner, a[n, lo:hi, hi:], ((1,), (0,)))
                        a[n, hi:, hi:] -= dot3(right, right, ((0,), (0,)))
                        x[n, hi:, :hi] -= dot3(right, x[n, lo:hi, :hi], ((0,), (0,)))

    for n in many:
        o_ref[n] = x[n].T * jnp.float32(total_rows)


def inverse_kernel(total_rows, g_ref, o_ref, a, x):
    inverse_of(total_rows, g_ref, o_ref, a, x, range(a.shape[0]))


def invert(g, width, total_rows):
    layers = g.shape[0]
    return pl.pallas_call(
        lambda *refs: inverse_kernel(total_rows, *refs),
        in_specs=[pl.BlockSpec(memory_space=pltpu.VMEM)],
        out_specs=pl.BlockSpec(memory_space=pltpu.VMEM),
        out_shape=jax.ShapeDtypeStruct((layers, width, width), jnp.float32),
        scratch_shapes=[pltpu.VMEM((layers, width, width), jnp.float32)] * 2,
        compiler_params=pltpu.CompilerParams(vmem_limit_bytes=40 * 2**20),
        cost_estimate=pl.CostEstimate(
            flops=40 * 10**9, bytes_accessed=8 * width * width, transcendentals=0
        ),
        name="invert",
    )(g)


def apply_kernel(r_ref, u_ref, o_ref):
    o_ref[0] = dot3(r_ref[0], u_ref[0], ((1,), (0,)))


def apply(rows_here, upper):
    layers, row_count, width = rows_here.shape
    tile = min(256, row_count)
    while row_count % tile:
        tile -= 8
    return pl.pallas_call(
        apply_kernel,
        grid=(layers, row_count // tile),
        in_specs=[
            pl.BlockSpec((1, tile, width), lambda l, i: (l, i, 0)),
            pl.BlockSpec((1, width, width), lambda l, i: (l, 0, 0)),
        ],
        out_specs=pl.BlockSpec((1, tile, width), lambda l, i: (l, i, 0)),
        out_shape=jax.ShapeDtypeStruct((layers, row_count, width), jnp.float32),
        compiler_params=pltpu.CompilerParams(vmem_limit_bytes=40 * 2**20),
        cost_estimate=pl.CostEstimate(
            flops=6 * layers * row_count * width * width,
            bytes_accessed=8 * layers * row_count * width,
            transcendentals=0,
        ),
        name="apply",
    )(rows_here, upper)


MESH = pl.DeviceIdType.MESH


def remote(src, dst, send, recv, device):
    return pltpu.make_async_remote_copy(
        src_ref=src, dst_ref=dst, send_sem=send, recv_sem=recv, device_id=device, device_id_type=MESH
    )


def fused_kernel(
    cols, chips, total_rows, keep_ref, w_ref, s_ref, rows_ref, u_ref,
    g_ref, a, x, wbuf, part, inbox, pack, pair, box, full,
    wsem, rs_send, rs_recv, pair_send, pair_recv, out_send, out_recv, all_send, all_recv,
    back_send, back_recv,
):
    row, col = lax.axis_index("row"), lax.axis_index("col")
    core, z = row % 2, row // 2
    cx, cy = col % 2, col // 2
    me = z * cols + col
    half = wbuf.shape[1]
    width = s_ref.shape[1]
    blocks = half // BLOCK
    share = pack.shape[1] // 2
    piece = share // chips
    to_x = (row, cy * 2 + (1 - cx))
    to_y = (row, (1 - cy) * 2 + cx)
    partner = (row + 1 - 2 * core, col)

    def peer(offset):
        p = (me + offset) % chips
        return p, ((p // cols) * 2 + core, p % cols)

    barrier = pltpu.get_barrier_semaphore()
    pl.semaphore_signal(barrier, inc=1, device_id=partner, device_id_type=MESH)
    for offset in range(1, chips):
        pl.semaphore_signal(barrier, inc=1, device_id=peer(offset)[1], device_id_type=MESH)

    slots = [(1, 1, 0), (1, 1, 1), (1, 0, 0), (0, 1, 1), (0, 1, 0), (1, 0, 1), (0, 0, 0), (0, 0, 1)]

    def first_block(slot):
        dx, dy, part_of = slots[slot]
        owner = ((cy + dy) % 2) * 2 + (cx + dx) % 2
        return (owner * 2 + part_of) * blocks

    def fetch(step):
        layer, slot = step // 8, step % 8
        start = pl.multiple_of(first_block(slot) * BLOCK, BLOCK)
        return pltpu.make_async_copy(
            w_ref.at[layer, pl.ds(start, half)], wbuf.at[step % 2], wsem.at[step % 2]
        )

    def product(step):
        layer, slot = step // 8, step % 8
        if step + 1 < 8 * LAYERS:
            fetch(step + 1).start()
        fetch(step).wait()
        first = first_block(slot)
        kept = [
            wbuf[step % 2, b * BLOCK : (b + 1) * BLOCK, :] * keep_ref[layer, first + b]
            for b in range(blocks)
        ]
        part[layer, slot] = jnp.dot(
            jnp.concatenate(kept, axis=0), s_ref[...], preferred_element_type=jnp.float32
        )

    targets = [to_x, to_y, to_x, to_y, to_y, to_x]

    def hop(layer, k):
        return remote(
            part.at[layer, k], inbox.at[layer, k],
            rs_send.at[layer, k], rs_recv.at[layer, k], targets[k],
        )

    def combine(layer):
        for k in (0, 1):
            hop(layer, k).wait_recv()
            part[layer, 4 + k] += inbox[layer, k]
            hop(layer, 4 + k).start()

    def gather_rows(layer):
        for k in (0, 1):
            hop(layer, 2 + k).wait_recv()
            hop(layer, 4 + k).wait_recv()
            rows_ref[layer, k * half : (k + 1) * half] = (
                part[layer, 6 + k] + inbox[layer, 2 + k] + inbox[layer, 4 + k]
            )

    def gram(layer):
        at = 0
        for i in range(width // BLOCK):
            lo = i * BLOCK
            g = dot3(
                rows_ref[layer, :, lo : lo + BLOCK], rows_ref[layer, :, lo:], ((0,), (0,))
            )
            for j in range((width - lo) // BLOCK):
                pack[layer, at : at + BLOCK] = g[:, j * BLOCK : (j + 1) * BLOCK]
                at += BLOCK

    def pair_copy(layer):
        other = pl.ds(pl.multiple_of((1 - core) * share, 8), share)
        return remote(
            pack.at[layer, other], pair.at[layer],
            pair_send.at[layer], pair_recv.at[layer], partner,
        )

    def out_copy(layer, offset):
        p, device = peer(offset)
        mine = pl.ds(pl.multiple_of(core * share + p * piece, 8), piece)
        return remote(
            pack.at[layer, mine], box.at[layer, offset],
            out_send.at[layer, offset], out_recv.at[layer, offset], device,
        )

    def all_copy(layer, offset):
        device = peer(offset)[1]
        here = full.at[layer, core, pl.ds(pl.multiple_of(me * piece, 8), piece)]
        return remote(
            here, here, all_send.at[layer, offset], all_recv.at[layer, offset], device
        )

    def back_copy(layer):
        here = full.at[layer, core]
        return remote(here, here, back_send.at[layer], back_recv.at[layer], partner)

    def sum_start(layer):
        pair_copy(layer).start()
        pair_copy(layer).wait_recv()
        own = pl.ds(pl.multiple_of(core * share, 8), share)
        pack[layer, own] += pair[layer]
        for offset in range(1, chips):
            out_copy(layer, offset).start()

    def sum_middle(layer):
        mine = pl.ds(pl.multiple_of(core * share + me * piece, 8), piece)
        total = pack[layer, mine]
        for offset in range(1, chips):
            out_copy(layer, offset).wait_recv()
            total = total + box[layer, offset]
        full[layer, core, pl.ds(pl.multiple_of(me * piece, 8), piece)] = total
        for offset in range(1, chips):
            all_copy(layer, offset).start()

    def sum_end(layer):
        for offset in range(1, chips):
            all_copy(layer, offset).wait_recv()
        back_copy(layer).start()
        back_copy(layer).wait_recv()
        for c in range(2):
            g_ref[layer, c * share : (c + 1) * share] = full[layer, c]

    fetch(0).start()
    for slot in range(8):
        product(slot)
        if slot == 0:
            pl.semaphore_wait(barrier, chips)
        if slot < 4:
            hop(0, slot).start()
    for slot in range(4):
        product(8 + slot)
    combine(0)
    for k in (0, 1):
        hop(1, k).start()
    for slot in range(4, 8):
        product(8 + slot)
    gather_rows(0)
    gram(0)
    sum_start(0)
    combine(1)
    sum_middle(0)
    for k in (2, 3):
        hop(1, k).start()
    sum_end(0)
    inverse_of(total_rows, g_ref, u_ref, a, x, [0])
    gather_rows(1)
    gram(1)
    sum_start(1)
    sum_middle(1)
    sum_end(1)
    inverse_of(total_rows, g_ref, u_ref, a, x, [1])

    for layer in range(LAYERS):
        for k in range(6):
            hop(layer, k).wait_send()
        pair_copy(layer).wait_send()
        back_copy(layer).wait_send()
        for offset in range(1, chips):
            out_copy(layer, offset).wait_send()
            all_copy(layer, offset).wait_send()


def fused(weights, keep, sketch, cols, chips, total_rows):
    _, row_count, col_count = weights.shape
    width = sketch.shape[1]
    rows_here = row_count // cols
    half = rows_here // 2
    packed = len(upper_blocks(width)) * BLOCK
    share = packed // 2
    vmem = pl.BlockSpec(memory_space=pltpu.VMEM)
    f32 = jnp.float32
    dma = pltpu.SemaphoreType.DMA
    return pl.pallas_call(
        lambda *refs: fused_kernel(cols, chips, total_rows, *refs),
        in_specs=[vmem, pl.BlockSpec(memory_space=pl.ANY), vmem],
        out_specs=[vmem, vmem],
        out_shape=[
            jax.ShapeDtypeStruct((LAYERS, rows_here, width), f32),
            jax.ShapeDtypeStruct((LAYERS, width, width), f32),
        ],
        scratch_shapes=[
            pltpu.VMEM((LAYERS, packed, BLOCK), f32),
            pltpu.VMEM((LAYERS, width, width), f32),
            pltpu.VMEM((LAYERS, width, width), f32),
            pltpu.VMEM((2, half, col_count), jnp.bfloat16),
            pltpu.VMEM((LAYERS, 8, half, width), f32),
            pltpu.VMEM((LAYERS, 6, half, width), f32),
            pltpu.VMEM((LAYERS, packed, BLOCK), f32),
            pltpu.VMEM((LAYERS, share, BLOCK), f32),
            pltpu.VMEM((LAYERS, chips, share // chips, BLOCK), f32),
            pltpu.VMEM((LAYERS, 2, share, BLOCK), f32),
            dma((2,)),
            dma((LAYERS, 6)),
            dma((LAYERS, 6)),
            dma((LAYERS,)),
            dma((LAYERS,)),
            dma((LAYERS, chips)),
            dma((LAYERS, chips)),
            dma((LAYERS, chips)),
            dma((LAYERS, chips)),
            dma((LAYERS,)),
            dma((LAYERS,)),
        ],
        compiler_params=pltpu.CompilerParams(
            vmem_limit_bytes=56 * 2**20, collective_id=0, has_side_effects=True
        ),
        cost_estimate=pl.CostEstimate(
            flops=2 * LAYERS * row_count * col_count * width,
            bytes_accessed=2 * LAYERS * row_count * col_count,
            transcendentals=0,
        ),
        name="fused",
    )(keep, weights, sketch)


def local_gram(rows_here):
    return lax.dot_general(
        rows_here,
        rows_here,
        (((0,), (0,)), ((), ())),
        precision=lax.Precision.HIGH,
        preferred_element_type=jnp.float32,
    )


def make_body(mesh):
    rows, cols = mesh.shape["row"], mesh.shape["col"]
    chips = rows // 2 * cols

    def body(weights, pattern, sketch):
        total_rows = weights.shape[1] * rows
        width = sketch.shape[1]
        blocks = upper_blocks(width)
        keep = jnp.repeat((1 - pattern).astype(jnp.bfloat16), BLOCK, axis=2)[:, :, None, :]
        if cols == 4 and rows % 2 == 0 and (len(blocks) * BLOCK) % (2 * chips * 8) == 0:
            sampled, upper = fused(weights, keep, sketch, cols, chips, total_rows)
        else:
            sampled = jnp.stack(
                [
                    lax.psum_scatter(
                        sample(weights, keep, sketch, layer), "col", scatter_dimension=0, tiled=True
                    )
                    for layer in range(LAYERS)
                ]
            )
            g = [local_gram(sampled[layer]) for layer in range(LAYERS)]
            packed = jnp.stack(
                [
                    jnp.concatenate(
                        [
                            x[i * BLOCK : (i + 1) * BLOCK, j * BLOCK : (j + 1) * BLOCK]
                            for i, j in blocks
                        ]
                    )
                    for x in g
                ]
            )
            gram = lax.psum(packed, ("row", "col"))
            upper = invert(gram, width, total_rows)
        return apply(sampled, upper)

    return body


def solution(mesh):
    return jax.shard_map(
        make_body(mesh),
        mesh=mesh,
        in_specs=(P(None, "row", "col"), P(None, "row", "col"), P("col", None)),
        out_specs=P(None, ("row", "col"), None),
        check_vma=False,
    )
```

```python
import jax
import jax.numpy as jnp
from jax import lax
from jax.experimental import pallas as pl
from jax.experimental.pallas import tpu as pltpu
from jax.sharding import PartitionSpec as P

BLOCK = 128
LAYERS = 2
GROUP = 8


def split(x):
    high = x.astype(jnp.bfloat16)
    low = (x - high.astype(jnp.float32)).astype(jnp.bfloat16)
    return high, low


def dot3(a, b, dims):
    a_high, a_low = split(a)
    b_high, b_low = split(b)

    def one(x, y):
        return lax.dot_general(x, y, (dims, ((), ())), preferred_element_type=jnp.float32)

    return one(a_high, b_high) + (one(a_high, b_low) + one(a_low, b_high))


def sample_kernel(keep_ref, w_ref, s_ref, o_ref):
    rows = w_ref.shape[1]
    parts = []
    for block in range(rows // BLOCK):
        parts.append(w_ref[0, block * BLOCK : (block + 1) * BLOCK, :] * keep_ref[0, block])
    leftover = jnp.concatenate(parts, axis=0)
    o_ref[...] = jnp.dot(leftover, s_ref[...], preferred_element_type=jnp.float32)


def sample(weights, keep, sketch, layer):
    _, row_count, col_count = weights.shape
    width = sketch.shape[1]
    tile = min(512, row_count)
    while row_count % tile:
        tile -= BLOCK
    return pl.pallas_call(
        sample_kernel,
        grid=(row_count // tile,),
        in_specs=[
            pl.BlockSpec((1, tile // BLOCK, 1, col_count), lambda i: (layer, i, 0, 0)),
            pl.BlockSpec((1, tile, col_count), lambda i: (layer, i, 0)),
            pl.BlockSpec((col_count, width), lambda i: (0, 0)),
        ],
        out_specs=pl.BlockSpec((tile, width), lambda i: (i, 0)),
        out_shape=jax.ShapeDtypeStruct((row_count, width), jnp.float32),
        compiler_params=pltpu.CompilerParams(vmem_limit_bytes=40 * 2**20),
        cost_estimate=pl.CostEstimate(
            flops=2 * row_count * col_count * width,
            bytes_accessed=2 * row_count * col_count + 4 * row_count * width,
            transcendentals=0,
        ),
        name="sample",
    )(keep, weights, sketch)


def factor_blocks(blocks, size):
    many = range(len(blocks))
    row = lax.broadcasted_iota(jnp.int32, (size, size), 0)
    col = lax.broadcasted_iota(jnp.int32, (size, size), 1)
    eye = (row == col).astype(jnp.float32)
    sub = lax.broadcasted_iota(jnp.int32, (GROUP, size), 0)
    d = list(blocks)
    e = [eye for _ in many]
    done = [[] for _ in many]
    for start in range(0, size, GROUP):
        live = size - start
        cols = [
            [
                jnp.broadcast_to(d[n][:, start + k : start + k + 1], (live, size))
                for k in range(GROUP)
            ]
            for n in many
        ]
        head_cols = [[c[:GROUP] for c in cols[n]] for n in many]
        tail_cols = [[c[GROUP:] for c in cols[n]] for n in many]
        head_d, tail_d = [x[:GROUP] for x in d], [x[GROUP:] for x in d]
        head_e, tail_e = [x[:GROUP] for x in e], [x[GROUP:] for x in e]
        scale = [jnp.zeros((GROUP, size), jnp.float32) for _ in many]
        for k in range(GROUP):
            for n in many:
                pivot = head_cols[n][k][k : k + 1]
                inverse = 1.0 / pivot
                scale[n] = jnp.where(sub == k, lax.rsqrt(pivot), scale[n])
                factor = jnp.where(sub > k, head_cols[n][k], 0.0)
                row_e = head_e[n][k : k + 1] * inverse
                row_d = head_d[n][k : k + 1] * inverse
                for j in range(k + 1, GROUP):
                    step = head_cols[n][j][k : k + 1] * inverse
                    head_cols[n][j] = head_cols[n][j] - factor * step
                    if live > GROUP:
                        tail_cols[n][j] = tail_cols[n][j] - tail_cols[n][k] * step
                head_d[n] = head_d[n] - factor * row_d
                head_e[n] = head_e[n] - factor * row_e
                if live > GROUP:
                    tail_d[n] = tail_d[n] - tail_cols[n][k] * row_d
                    tail_e[n] = tail_e[n] - tail_cols[n][k] * row_e
        for n in many:
            done[n].append(head_e[n] * scale[n])
        d, e = tail_d, tail_e
    return [jnp.concatenate(done[n], axis=0) for n in many]


def upper_blocks(width):
    count = width // BLOCK
    return [(i, j) for i in range(count) for j in range(i, count)]


def inverse_of(g_ref, a, x, many):
    width = a.shape[1]
    count = width // BLOCK
    for n in many:
        a[n] = jnp.zeros((width, width), jnp.float32)
        x[n] = jnp.zeros((width, width), jnp.float32)
        for b, (i, j) in enumerate(upper_blocks(width)):
            a[n, i * BLOCK : (i + 1) * BLOCK, j * BLOCK : (j + 1) * BLOCK] = g_ref[
                n, b * BLOCK : (b + 1) * BLOCK
            ]

    @pl.loop(0, count)
    def _(k):
        here = pl.ds(pl.multiple_of(k * BLOCK, BLOCK), BLOCK)
        inners = factor_blocks([a[n, here, here] for n in many], BLOCK)
        for now in range(count):

            @pl.when(k == now)
            def _():
                lo, hi = now * BLOCK, (now + 1) * BLOCK
                for n, inner in zip(many, inners):
                    if now:
                        x[n, lo:hi, :lo] = dot3(inner, x[n, lo:hi, :lo], ((1,), (0,)))
                    x[n, lo:hi, lo:hi] = inner
                    if now < count - 1:
                        right = dot3(inner, a[n, lo:hi, hi:], ((1,), (0,)))
                        a[n, hi:, hi:] -= dot3(right, right, ((0,), (0,)))
                        x[n, hi:, :hi] -= dot3(right, x[n, lo:hi, :hi], ((0,), (0,)))


def inverse_kernel(total_rows, g_ref, o_ref, a, x):
    inverse_of(g_ref, a, x, range(a.shape[0]))
    for n in range(a.shape[0]):
        o_ref[n] = x[n].T * jnp.float32(total_rows)


def invert(g, width, total_rows):
    layers = g.shape[0]
    return pl.pallas_call(
        lambda *refs: inverse_kernel(total_rows, *refs),
        in_specs=[pl.BlockSpec(memory_space=pltpu.VMEM)],
        out_specs=pl.BlockSpec(memory_space=pltpu.VMEM),
        out_shape=jax.ShapeDtypeStruct((layers, width, width), jnp.float32),
        scratch_shapes=[pltpu.VMEM((layers, width, width), jnp.float32)] * 2,
        compiler_params=pltpu.CompilerParams(vmem_limit_bytes=40 * 2**20),
        cost_estimate=pl.CostEstimate(
            flops=40 * 10**9, bytes_accessed=8 * width * width, transcendentals=0
        ),
        name="invert",
    )(g)


def apply_kernel(r_ref, u_ref, o_ref):
    o_ref[0] = dot3(r_ref[0], u_ref[0], ((1,), (0,)))


def apply(rows_here, upper):
    layers, row_count, width = rows_here.shape
    tile = min(256, row_count)
    while row_count % tile:
        tile -= 8
    return pl.pallas_call(
        apply_kernel,
        grid=(layers, row_count // tile),
        in_specs=[
            pl.BlockSpec((1, tile, width), lambda l, i: (l, i, 0)),
            pl.BlockSpec((1, width, width), lambda l, i: (l, 0, 0)),
        ],
        out_specs=pl.BlockSpec((1, tile, width), lambda l, i: (l, i, 0)),
        out_shape=jax.ShapeDtypeStruct((layers, row_count, width), jnp.float32),
        compiler_params=pltpu.CompilerParams(vmem_limit_bytes=40 * 2**20),
        cost_estimate=pl.CostEstimate(
            flops=6 * layers * row_count * width * width,
            bytes_accessed=8 * layers * row_count * width,
            transcendentals=0,
        ),
        name="apply",
    )(rows_here, upper)


MESH = pl.DeviceIdType.MESH


def remote(src, dst, send, recv, device):
    return pltpu.make_async_remote_copy(
        src_ref=src, dst_ref=dst, send_sem=send, recv_sem=recv, device_id=device, device_id_type=MESH
    )


def fused_kernel(
    cols, chips, total_rows, keep_ref, w_ref, s_ref, o_ref,
    rows_ref, basis, g_ref, a, x, wbuf, part, inbox, pack, pair, box, full,
    osem, wsem, rs_send, rs_recv, pair_send, pair_recv, out_send, out_recv, all_send, all_recv,
    back_send, back_recv,
):
    row, col = lax.axis_index("row"), lax.axis_index("col")
    core, z = row % 2, row // 2
    cx, cy = col % 2, col // 2
    me = z * cols + col
    half = wbuf.shape[1]
    width = s_ref.shape[1]
    blocks = half // BLOCK
    share = pack.shape[1] // 2
    piece = share // chips
    to_x = (row, cy * 2 + (1 - cx))
    to_y = (row, (1 - cy) * 2 + cx)
    partner = (row + 1 - 2 * core, col)

    def peer(offset):
        p = (me + offset) % chips
        return p, ((p // cols) * 2 + core, p % cols)

    barrier = pltpu.get_barrier_semaphore()
    pl.semaphore_signal(barrier, inc=1, device_id=partner, device_id_type=MESH)
    for offset in range(1, chips):
        pl.semaphore_signal(barrier, inc=1, device_id=peer(offset)[1], device_id_type=MESH)

    slots = [(1, 1, 0), (1, 1, 1), (1, 0, 0), (0, 1, 1), (0, 1, 0), (1, 0, 1), (0, 0, 0), (0, 0, 1)]

    def first_block(slot):
        dx, dy, part_of = slots[slot]
        owner = ((cy + dy) % 2) * 2 + (cx + dx) % 2
        return (owner * 2 + part_of) * blocks

    def fetch(step):
        layer, slot = step // 8, step % 8
        start = pl.multiple_of(first_block(slot) * BLOCK, BLOCK)
        return pltpu.make_async_copy(
            w_ref.at[layer, pl.ds(start, half)], wbuf.at[step % 2], wsem.at[step % 2]
        )

    def product(step):
        layer, slot = step // 8, step % 8
        if step + 1 < 8 * LAYERS:
            fetch(step + 1).start()
        fetch(step).wait()
        first = first_block(slot)
        kept = [
            wbuf[step % 2, b * BLOCK : (b + 1) * BLOCK, :] * keep_ref[layer, first + b]
            for b in range(blocks)
        ]
        part[layer, slot] = jnp.dot(
            jnp.concatenate(kept, axis=0), s_ref[...], preferred_element_type=jnp.float32
        )

    targets = [to_x, to_y, to_x, to_y, to_y, to_x]

    def hop(layer, k, b):
        here = pl.ds(b * BLOCK, BLOCK)
        return remote(
            part.at[layer, k, here], inbox.at[layer, k, here],
            rs_send.at[layer, k, b], rs_recv.at[layer, k, b], targets[k],
        )

    def combine(layer):
        for b in range(blocks):
            here = slice(b * BLOCK, (b + 1) * BLOCK)
            for k in (0, 1):
                hop(layer, k, b).wait_recv()
                part[layer, 4 + k, here] += inbox[layer, k, here]
                hop(layer, 4 + k, b).start()

    def gram(layer):
        for b in range(blocks):
            here = slice(b * BLOCK, (b + 1) * BLOCK)
            landed = []
            for k in (0, 1):
                hop(layer, 2 + k, b).wait_recv()
                hop(layer, 4 + k, b).wait_recv()
                landed.append(
                    part[layer, 6 + k, here] + inbox[layer, 2 + k, here] + inbox[layer, 4 + k, here]
                )
                first = k * half + b * BLOCK
                rows_ref[layer, first : first + BLOCK] = landed[k]
            y = jnp.concatenate(landed, axis=0)
            at = 0
            for i in range(width // BLOCK):
                lo = i * BLOCK
                g = dot3(y[:, lo : lo + BLOCK], y[:, lo:], ((0,), (0,)))
                for j in range((width - lo) // BLOCK):
                    term = g[:, j * BLOCK : (j + 1) * BLOCK]
                    if b:
                        term = term + pack[layer, at : at + BLOCK]
                    pack[layer, at : at + BLOCK] = term
                    at += BLOCK

    def out(layer):
        return pltpu.make_async_copy(basis.at[layer], o_ref.at[layer], osem.at[layer])

    def finish(layer):
        inverse_of(g_ref, a, x, [layer])
        high, low = split(x[layer])
        tile = 2 * BLOCK
        for first in range(0, 2 * half, tile):
            y_high, y_low = split(rows_ref[layer, first : first + tile])

            def one(p, q):
                return lax.dot_general(
                    p, q, (((1,), (1,)), ((), ())), preferred_element_type=jnp.float32
                )

            solved = one(y_high, high) + (one(y_high, low) + one(y_low, high))
            basis[layer, first : first + tile] = solved * jnp.float32(total_rows)
        out(layer).start()

    def pair_copy(layer):
        other = pl.ds(pl.multiple_of((1 - core) * share, 8), share)
        return remote(
            pack.at[layer, other], pair.at[layer],
            pair_send.at[layer], pair_recv.at[layer], partner,
        )

    def out_copy(layer, offset):
        p, device = peer(offset)
        mine = pl.ds(pl.multiple_of(core * share + p * piece, 8), piece)
        return remote(
            pack.at[layer, mine], box.at[layer, offset],
            out_send.at[layer, offset], out_recv.at[layer, offset], device,
        )

    def all_copy(layer, offset):
        device = peer(offset)[1]
        here = full.at[layer, core, pl.ds(pl.multiple_of(me * piece, 8), piece)]
        return remote(
            here, here, all_send.at[layer, offset], all_recv.at[layer, offset], device
        )

    def back_copy(layer):
        here = full.at[layer, core]
        return remote(here, here, back_send.at[layer], back_recv.at[layer], partner)

    def sum_start(layer):
        pair_copy(layer).start()
        pair_copy(layer).wait_recv()
        own = pl.ds(pl.multiple_of(core * share, 8), share)
        pack[layer, own] += pair[layer]
        for offset in range(1, chips):
            out_copy(layer, offset).start()

    def sum_middle(layer):
        mine = pl.ds(pl.multiple_of(core * share + me * piece, 8), piece)
        total = pack[layer, mine]
        for offset in range(1, chips):
            out_copy(layer, offset).wait_recv()
            total = total + box[layer, offset]
        full[layer, core, pl.ds(pl.multiple_of(me * piece, 8), piece)] = total
        for offset in range(1, chips):
            all_copy(layer, offset).start()

    def sum_end(layer):
        for offset in range(1, chips):
            all_copy(layer, offset).wait_recv()
        back_copy(layer).start()
        back_copy(layer).wait_recv()
        for c in range(2):
            g_ref[layer, c * share : (c + 1) * share] = full[layer, c]

    fetch(0).start()
    for slot in range(8):
        product(slot)
        if slot == 0:
            pl.semaphore_wait(barrier, chips)
        if slot < 4:
            for b in range(blocks):
                hop(0, slot, b).start()
    for slot in range(4):
        product(8 + slot)
    combine(0)
    for b in range(blocks):
        for k in (0, 1):
            hop(1, k, b).start()
    for slot in range(4, 8):
        product(8 + slot)
    gram(0)
    sum_start(0)
    combine(1)
    sum_middle(0)
    for b in range(blocks):
        for k in (2, 3):
            hop(1, k, b).start()
    sum_end(0)
    finish(0)
    gram(1)
    sum_start(1)
    sum_middle(1)
    sum_end(1)
    finish(1)

    for layer in range(LAYERS):
        for k in range(6):
            for b in range(blocks):
                hop(layer, k, b).wait_send()
        out(layer).wait()
        pair_copy(layer).wait_send()
        back_copy(layer).wait_send()
        for offset in range(1, chips):
            out_copy(layer, offset).wait_send()
            all_copy(layer, offset).wait_send()


def fused(weights, keep, sketch, cols, chips, total_rows):
    _, row_count, col_count = weights.shape
    width = sketch.shape[1]
    rows_here = row_count // cols
    half = rows_here // 2
    packed = len(upper_blocks(width)) * BLOCK
    share = packed // 2
    vmem = pl.BlockSpec(memory_space=pltpu.VMEM)
    f32 = jnp.float32
    dma = pltpu.SemaphoreType.DMA
    return pl.pallas_call(
        lambda *refs: fused_kernel(cols, chips, total_rows, *refs),
        in_specs=[vmem, pl.BlockSpec(memory_space=pl.ANY), vmem],
        out_specs=pl.BlockSpec(memory_space=pl.ANY),
        out_shape=jax.ShapeDtypeStruct((LAYERS, rows_here, width), f32),
        scratch_shapes=[
            pltpu.VMEM((LAYERS, rows_here, width), f32),
            pltpu.VMEM((LAYERS, rows_here, width), f32),
            pltpu.VMEM((LAYERS, packed, BLOCK), f32),
            pltpu.VMEM((LAYERS, width, width), f32),
            pltpu.VMEM((LAYERS, width, width), f32),
            pltpu.VMEM((2, half, col_count), jnp.bfloat16),
            pltpu.VMEM((LAYERS, 8, half, width), f32),
            pltpu.VMEM((LAYERS, 6, half, width), f32),
            pltpu.VMEM((LAYERS, packed, BLOCK), f32),
            pltpu.VMEM((LAYERS, share, BLOCK), f32),
            pltpu.VMEM((LAYERS, chips, share // chips, BLOCK), f32),
            pltpu.VMEM((LAYERS, 2, share, BLOCK), f32),
            dma((LAYERS,)),
            dma((2,)),
            dma((LAYERS, 6, half // BLOCK)),
            dma((LAYERS, 6, half // BLOCK)),
            dma((LAYERS,)),
            dma((LAYERS,)),
            dma((LAYERS, chips)),
            dma((LAYERS, chips)),
            dma((LAYERS, chips)),
            dma((LAYERS, chips)),
            dma((LAYERS,)),
            dma((LAYERS,)),
        ],
        compiler_params=pltpu.CompilerParams(
            vmem_limit_bytes=56 * 2**20, collective_id=0, has_side_effects=True
        ),
        cost_estimate=pl.CostEstimate(
            flops=2 * LAYERS * row_count * col_count * width,
            bytes_accessed=2 * LAYERS * row_count * col_count,
            transcendentals=0,
        ),
        name="fused",
    )(keep, weights, sketch)


def local_gram(rows_here):
    return lax.dot_general(
        rows_here,
        rows_here,
        (((0,), (0,)), ((), ())),
        precision=lax.Precision.HIGH,
        preferred_element_type=jnp.float32,
    )


def make_body(mesh):
    rows, cols = mesh.shape["row"], mesh.shape["col"]
    chips = rows // 2 * cols

    def body(weights, pattern, sketch):
        total_rows = weights.shape[1] * rows
        width = sketch.shape[1]
        blocks = upper_blocks(width)
        keep = jnp.repeat((1 - pattern).astype(jnp.bfloat16), BLOCK, axis=2)[:, :, None, :]
        if cols == 4 and rows % 2 == 0 and (len(blocks) * BLOCK) % (2 * chips * 8) == 0:
            return fused(weights, keep, sketch, cols, chips, total_rows)
        sampled = jnp.stack(
            [
                lax.psum_scatter(
                    sample(weights, keep, sketch, layer), "col", scatter_dimension=0, tiled=True
                )
                for layer in range(LAYERS)
            ]
        )
        g = [local_gram(sampled[layer]) for layer in range(LAYERS)]
        packed = jnp.stack(
            [
                jnp.concatenate(
                    [
                        x[i * BLOCK : (i + 1) * BLOCK, j * BLOCK : (j + 1) * BLOCK]
                        for i, j in blocks
                    ]
                )
                for x in g
            ]
        )
        gram = lax.psum(packed, ("row", "col"))
        upper = invert(gram, width, total_rows)
        return apply(sampled, upper)

    return body


def solution(mesh):
    return jax.shard_map(
        make_body(mesh),
        mesh=mesh,
        in_specs=(P(None, "row", "col"), P(None, "row", "col"), P("col", None)),
        out_specs=P(None, ("row", "col"), None),
        check_vma=False,
    )
```

```python
import jax
import jax.numpy as jnp
from jax import lax
from jax.experimental import pallas as pl
from jax.experimental.pallas import tpu as pltpu
from jax.sharding import PartitionSpec as P

BLOCK = 128
LAYERS = 2
GROUP = 8


def split(x):
    high = x.astype(jnp.bfloat16)
    low = (x - high.astype(jnp.float32)).astype(jnp.bfloat16)
    return high, low


def dot3(a, b, dims):
    a_high, a_low = split(a)
    b_high, b_low = split(b)

    def one(x, y):
        return lax.dot_general(x, y, (dims, ((), ())), preferred_element_type=jnp.float32)

    return one(a_high, b_high) + (one(a_high, b_low) + one(a_low, b_high))


def sample_kernel(keep_ref, w_ref, s_ref, o_ref):
    rows = w_ref.shape[1]
    parts = []
    for block in range(rows // BLOCK):
        parts.append(w_ref[0, block * BLOCK : (block + 1) * BLOCK, :] * keep_ref[0, block])
    leftover = jnp.concatenate(parts, axis=0)
    o_ref[...] = jnp.dot(leftover, s_ref[...], preferred_element_type=jnp.float32)


def sample(weights, keep, sketch, layer):
    _, row_count, col_count = weights.shape
    width = sketch.shape[1]
    tile = min(512, row_count)
    while row_count % tile:
        tile -= BLOCK
    return pl.pallas_call(
        sample_kernel,
        grid=(row_count // tile,),
        in_specs=[
            pl.BlockSpec((1, tile // BLOCK, 1, col_count), lambda i: (layer, i, 0, 0)),
            pl.BlockSpec((1, tile, col_count), lambda i: (layer, i, 0)),
            pl.BlockSpec((col_count, width), lambda i: (0, 0)),
        ],
        out_specs=pl.BlockSpec((tile, width), lambda i: (i, 0)),
        out_shape=jax.ShapeDtypeStruct((row_count, width), jnp.float32),
        compiler_params=pltpu.CompilerParams(vmem_limit_bytes=40 * 2**20),
        cost_estimate=pl.CostEstimate(
            flops=2 * row_count * col_count * width,
            bytes_accessed=2 * row_count * col_count + 4 * row_count * width,
            transcendentals=0,
        ),
        name="sample",
    )(keep, weights, sketch)


def factor_blocks(blocks, size):
    many = range(len(blocks))
    row = lax.broadcasted_iota(jnp.int32, (size, size), 0)
    col = lax.broadcasted_iota(jnp.int32, (size, size), 1)
    eye = (row == col).astype(jnp.float32)
    sub = lax.broadcasted_iota(jnp.int32, (GROUP, size), 0)
    d = list(blocks)
    e = [eye for _ in many]
    done = [[] for _ in many]
    for start in range(0, size, GROUP):
        live = size - start
        cols = [
            [
                jnp.broadcast_to(d[n][:, start + k : start + k + 1], (live, size))
                for k in range(GROUP)
            ]
            for n in many
        ]
        head_cols = [[c[:GROUP] for c in cols[n]] for n in many]
        tail_cols = [[c[GROUP:] for c in cols[n]] for n in many]
        head_d, tail_d = [x[:GROUP] for x in d], [x[GROUP:] for x in d]
        head_e, tail_e = [x[:GROUP] for x in e], [x[GROUP:] for x in e]
        scale = [jnp.zeros((GROUP, size), jnp.float32) for _ in many]
        for k in range(GROUP):
            for n in many:
                pivot = head_cols[n][k][k : k + 1]
                inverse = 1.0 / pivot
                scale[n] = jnp.where(sub == k, lax.rsqrt(pivot), scale[n])
                factor = jnp.where(sub > k, head_cols[n][k], 0.0)
                row_e = head_e[n][k : k + 1] * inverse
                row_d = head_d[n][k : k + 1] * inverse
                for j in range(k + 1, GROUP):
                    step = head_cols[n][j][k : k + 1] * inverse
                    head_cols[n][j] = head_cols[n][j] - factor * step
                    if live > GROUP:
                        tail_cols[n][j] = tail_cols[n][j] - tail_cols[n][k] * step
                head_d[n] = head_d[n] - factor * row_d
                head_e[n] = head_e[n] - factor * row_e
                if live > GROUP:
                    tail_d[n] = tail_d[n] - tail_cols[n][k] * row_d
                    tail_e[n] = tail_e[n] - tail_cols[n][k] * row_e
        for n in many:
            done[n].append(head_e[n] * scale[n])
        d, e = tail_d, tail_e
    return [jnp.concatenate(done[n], axis=0) for n in many]


def upper_blocks(width):
    count = width // BLOCK
    return [(i, j) for i in range(count) for j in range(i, count)]


def inverse_of(g_ref, a, x, many):
    width = a.shape[1]
    count = width // BLOCK
    for n in many:
        a[n] = jnp.zeros((width, width), jnp.float32)
        x[n] = jnp.zeros((width, width), jnp.float32)
        for b, (i, j) in enumerate(upper_blocks(width)):
            a[n, i * BLOCK : (i + 1) * BLOCK, j * BLOCK : (j + 1) * BLOCK] = g_ref[
                n, b * BLOCK : (b + 1) * BLOCK
            ]

    @pl.loop(0, count)
    def _(k):
        here = pl.ds(pl.multiple_of(k * BLOCK, BLOCK), BLOCK)
        inners = factor_blocks([a[n, here, here] for n in many], BLOCK)
        for now in range(count):

            @pl.when(k == now)
            def _():
                lo, hi = now * BLOCK, (now + 1) * BLOCK
                for n, inner in zip(many, inners):
                    if now:
                        x[n, lo:hi, :lo] = dot3(inner, x[n, lo:hi, :lo], ((1,), (0,)))
                    x[n, lo:hi, lo:hi] = inner
                    if now < count - 1:
                        right = dot3(inner, a[n, lo:hi, hi:], ((1,), (0,)))
                        a[n, hi:, hi:] -= dot3(right, right, ((0,), (0,)))
                        x[n, hi:, :hi] -= dot3(right, x[n, lo:hi, :hi], ((0,), (0,)))


def inverse_kernel(total_rows, g_ref, o_ref, a, x):
    inverse_of(g_ref, a, x, range(a.shape[0]))
    for n in range(a.shape[0]):
        o_ref[n] = x[n].T * jnp.float32(total_rows)


def invert(g, width, total_rows):
    layers = g.shape[0]
    return pl.pallas_call(
        lambda *refs: inverse_kernel(total_rows, *refs),
        in_specs=[pl.BlockSpec(memory_space=pltpu.VMEM)],
        out_specs=pl.BlockSpec(memory_space=pltpu.VMEM),
        out_shape=jax.ShapeDtypeStruct((layers, width, width), jnp.float32),
        scratch_shapes=[pltpu.VMEM((layers, width, width), jnp.float32)] * 2,
        compiler_params=pltpu.CompilerParams(vmem_limit_bytes=40 * 2**20),
        cost_estimate=pl.CostEstimate(
            flops=40 * 10**9, bytes_accessed=8 * width * width, transcendentals=0
        ),
        name="invert",
    )(g)


def apply_kernel(r_ref, u_ref, o_ref):
    o_ref[0] = dot3(r_ref[0], u_ref[0], ((1,), (0,)))


def apply(rows_here, upper):
    layers, row_count, width = rows_here.shape
    tile = min(256, row_count)
    while row_count % tile:
        tile -= 8
    return pl.pallas_call(
        apply_kernel,
        grid=(layers, row_count // tile),
        in_specs=[
            pl.BlockSpec((1, tile, width), lambda l, i: (l, i, 0)),
            pl.BlockSpec((1, width, width), lambda l, i: (l, 0, 0)),
        ],
        out_specs=pl.BlockSpec((1, tile, width), lambda l, i: (l, i, 0)),
        out_shape=jax.ShapeDtypeStruct((layers, row_count, width), jnp.float32),
        compiler_params=pltpu.CompilerParams(vmem_limit_bytes=40 * 2**20),
        cost_estimate=pl.CostEstimate(
            flops=6 * layers * row_count * width * width,
            bytes_accessed=8 * layers * row_count * width,
            transcendentals=0,
        ),
        name="apply",
    )(rows_here, upper)


MESH = pl.DeviceIdType.MESH


def remote(src, dst, send, recv, device):
    return pltpu.make_async_remote_copy(
        src_ref=src, dst_ref=dst, send_sem=send, recv_sem=recv, device_id=device, device_id_type=MESH
    )


def fused_kernel(
    cols, chips, total_rows, keep_ref, w_ref, s_ref, o_ref,
    rows_ref, basis, g_ref, a, x, wbuf, part, inbox, pack, pair, box, full,
    osem, wsem, rs_send, rs_recv, pair_send, pair_recv, out_send, out_recv, all_send, all_recv,
    back_send, back_recv,
):
    row, col = lax.axis_index("row"), lax.axis_index("col")
    core, z = row % 2, row // 2
    cx, cy = col % 2, col // 2
    me = z * cols + col
    half = wbuf.shape[1]
    width = s_ref.shape[1]
    blocks = half // BLOCK
    share = pack.shape[1] // 2
    piece = share // chips
    to_x = (row, cy * 2 + (1 - cx))
    to_y = (row, (1 - cy) * 2 + cx)
    partner = (row + 1 - 2 * core, col)

    def peer(offset):
        p = (me + offset) % chips
        return p, ((p // cols) * 2 + core, p % cols)

    barrier = pltpu.get_barrier_semaphore()
    pl.semaphore_signal(barrier, inc=1, device_id=partner, device_id_type=MESH)
    for offset in range(1, chips):
        pl.semaphore_signal(barrier, inc=1, device_id=peer(offset)[1], device_id_type=MESH)

    slots = [(1, 1, 0), (1, 1, 1), (1, 0, 0), (0, 1, 1), (0, 1, 0), (1, 0, 1), (0, 0, 0), (0, 0, 1)]

    def first_block(slot):
        dx, dy, part_of = slots[slot]
        owner = ((cy + dy) % 2) * 2 + (cx + dx) % 2
        return (owner * 2 + part_of) * blocks

    def fetch(step):
        layer, slot = step // 8, step % 8
        start = pl.multiple_of(first_block(slot) * BLOCK, BLOCK)
        return pltpu.make_async_copy(
            w_ref.at[layer, pl.ds(start, half)], wbuf.at[step % 2], wsem.at[step % 2]
        )

    def product(step):
        layer, slot = step // 8, step % 8
        if step + 1 < 8 * LAYERS:
            fetch(step + 1).start()
        fetch(step).wait()
        first = first_block(slot)
        kept = [
            wbuf[step % 2, b * BLOCK : (b + 1) * BLOCK, :] * keep_ref[layer, first + b]
            for b in range(blocks)
        ]
        part[layer, slot] = jnp.dot(
            jnp.concatenate(kept, axis=0), s_ref[...], preferred_element_type=jnp.float32
        )

    targets = [to_x, to_y, to_x, to_y, to_y, to_x]

    def hop(layer, k, b):
        here = pl.ds(b * BLOCK, BLOCK)
        return remote(
            part.at[layer, k, here], inbox.at[layer, k, here],
            rs_send.at[layer, k, b], rs_recv.at[layer, k, b], targets[k],
        )

    def combine(layer):
        for b in range(blocks):
            here = slice(b * BLOCK, (b + 1) * BLOCK)
            for k in (0, 1):
                hop(layer, k, b).wait_recv()
                part[layer, 4 + k, here] += inbox[layer, k, here]
                hop(layer, 4 + k, b).start()

    def gram(layer):
        for b in range(blocks):
            here = slice(b * BLOCK, (b + 1) * BLOCK)
            landed = []
            for k in (0, 1):
                hop(layer, 2 + k, b).wait_recv()
                hop(layer, 4 + k, b).wait_recv()
                landed.append(
                    part[layer, 6 + k, here] + inbox[layer, 2 + k, here] + inbox[layer, 4 + k, here]
                )
                first = k * half + b * BLOCK
                rows_ref[layer, first : first + BLOCK] = landed[k]
            y = jnp.concatenate(landed, axis=0)
            at = 0
            for i in range(width // BLOCK):
                lo = i * BLOCK
                g = dot3(y[:, lo : lo + BLOCK], y[:, lo:], ((0,), (0,)))
                for j in range((width - lo) // BLOCK):
                    term = g[:, j * BLOCK : (j + 1) * BLOCK]
                    if b:
                        term = term + pack[layer, at : at + BLOCK]
                    pack[layer, at : at + BLOCK] = term
                    at += BLOCK

    def out(layer):
        return pltpu.make_async_copy(basis.at[layer], o_ref.at[layer], osem.at[layer])

    def finish(layer):
        inverse_of(g_ref, a, x, [layer])
        high, low = split(x[layer])
        tile = 2 * BLOCK
        for first in range(0, 2 * half, tile):
            y_high, y_low = split(rows_ref[layer, first : first + tile])

            def one(p, q):
                return lax.dot_general(
                    p, q, (((1,), (1,)), ((), ())), preferred_element_type=jnp.float32
                )

            solved = one(y_high, high) + (one(y_high, low) + one(y_low, high))
            basis[layer, first : first + tile] = solved * jnp.float32(total_rows)
        out(layer).start()

    def pair_copy(layer):
        other = pl.ds(pl.multiple_of((1 - core) * share, 8), share)
        return remote(
            pack.at[layer, other], pair.at[layer],
            pair_send.at[layer], pair_recv.at[layer], partner,
        )

    def out_copy(layer, offset):
        p, device = peer(offset)
        mine = pl.ds(pl.multiple_of(core * share + p * piece, 8), piece)
        return remote(
            pack.at[layer, mine], box.at[layer, offset],
            out_send.at[layer, offset], out_recv.at[layer, offset], device,
        )

    def all_copy(layer, offset):
        device = peer(offset)[1]
        here = full.at[layer, core, pl.ds(pl.multiple_of(me * piece, 8), piece)]
        return remote(
            here, here, all_send.at[layer, offset], all_recv.at[layer, offset], device
        )

    def back_copy(layer):
        here = full.at[layer, core]
        return remote(here, here, back_send.at[layer], back_recv.at[layer], partner)

    def sum_start(layer):
        pair_copy(layer).start()
        pair_copy(layer).wait_recv()
        own = pl.ds(pl.multiple_of(core * share, 8), share)
        pack[layer, own] += pair[layer]
        for offset in range(1, chips):
            out_copy(layer, offset).start()

    def sum_middle(layer):
        mine = pl.ds(pl.multiple_of(core * share + me * piece, 8), piece)
        total = pack[layer, mine]
        for offset in range(1, chips):
            out_copy(layer, offset).wait_recv()
            total = total + box[layer, offset]
        full[layer, core, pl.ds(pl.multiple_of(me * piece, 8), piece)] = total
        for offset in range(1, chips):
            all_copy(layer, offset).start()

    def sum_end(layer):
        for offset in range(1, chips):
            all_copy(layer, offset).wait_recv()
        back_copy(layer).start()
        back_copy(layer).wait_recv()
        for c in range(2):
            g_ref[layer, c * share : (c + 1) * share] = full[layer, c]

    fetch(0).start()
    for slot in range(8):
        product(slot)
        if slot == 0:
            pl.semaphore_wait(barrier, chips)
        if slot < 4:
            for b in range(blocks):
                hop(0, slot, b).start()
    for slot in range(4):
        product(8 + slot)
    combine(0)
    for b in range(blocks):
        for k in (0, 1):
            hop(1, k, b).start()
    for slot in range(4, 8):
        product(8 + slot)
    for k in (2, 3):
        hop(1, k, 0).start()
    gram(0)
    sum_start(0)
    combine(1)
    sum_middle(0)
    for b in range(1, blocks):
        for k in (2, 3):
            hop(1, k, b).start()
    sum_end(0)
    finish(0)
    gram(1)
    sum_start(1)
    sum_middle(1)
    sum_end(1)
    finish(1)

    for layer in range(LAYERS):
        for k in range(6):
            for b in range(blocks):
                hop(layer, k, b).wait_send()
        out(layer).wait()
        pair_copy(layer).wait_send()
        back_copy(layer).wait_send()
        for offset in range(1, chips):
            out_copy(layer, offset).wait_send()
            all_copy(layer, offset).wait_send()


def fused(weights, keep, sketch, cols, chips, total_rows):
    _, row_count, col_count = weights.shape
    width = sketch.shape[1]
    rows_here = row_count // cols
    half = rows_here // 2
    packed = len(upper_blocks(width)) * BLOCK
    share = packed // 2
    vmem = pl.BlockSpec(memory_space=pltpu.VMEM)
    f32 = jnp.float32
    dma = pltpu.SemaphoreType.DMA
    return pl.pallas_call(
        lambda *refs: fused_kernel(cols, chips, total_rows, *refs),
        in_specs=[vmem, pl.BlockSpec(memory_space=pl.ANY), vmem],
        out_specs=pl.BlockSpec(memory_space=pl.ANY),
        out_shape=jax.ShapeDtypeStruct((LAYERS, rows_here, width), f32),
        scratch_shapes=[
            pltpu.VMEM((LAYERS, rows_here, width), f32),
            pltpu.VMEM((LAYERS, rows_here, width), f32),
            pltpu.VMEM((LAYERS, packed, BLOCK), f32),
            pltpu.VMEM((LAYERS, width, width), f32),
            pltpu.VMEM((LAYERS, width, width), f32),
            pltpu.VMEM((2, half, col_count), jnp.bfloat16),
            pltpu.VMEM((LAYERS, 8, half, width), f32),
            pltpu.VMEM((LAYERS, 6, half, width), f32),
            pltpu.VMEM((LAYERS, packed, BLOCK), f32),
            pltpu.VMEM((LAYERS, share, BLOCK), f32),
            pltpu.VMEM((LAYERS, chips, share // chips, BLOCK), f32),
            pltpu.VMEM((LAYERS, 2, share, BLOCK), f32),
            dma((LAYERS,)),
            dma((2,)),
            dma((LAYERS, 6, half // BLOCK)),
            dma((LAYERS, 6, half // BLOCK)),
            dma((LAYERS,)),
            dma((LAYERS,)),
            dma((LAYERS, chips)),
            dma((LAYERS, chips)),
            dma((LAYERS, chips)),
            dma((LAYERS, chips)),
            dma((LAYERS,)),
            dma((LAYERS,)),
        ],
        compiler_params=pltpu.CompilerParams(
            vmem_limit_bytes=56 * 2**20, collective_id=0, has_side_effects=True
        ),
        cost_estimate=pl.CostEstimate(
            flops=2 * LAYERS * row_count * col_count * width,
            bytes_accessed=2 * LAYERS * row_count * col_count,
            transcendentals=0,
        ),
        name="fused",
    )(keep, weights, sketch)


def local_gram(rows_here):
    return lax.dot_general(
        rows_here,
        rows_here,
        (((0,), (0,)), ((), ())),
        precision=lax.Precision.HIGH,
        preferred_element_type=jnp.float32,
    )


def make_body(mesh):
    rows, cols = mesh.shape["row"], mesh.shape["col"]
    chips = rows // 2 * cols

    def body(weights, pattern, sketch):
        total_rows = weights.shape[1] * rows
        width = sketch.shape[1]
        blocks = upper_blocks(width)
        keep = jnp.repeat((1 - pattern).astype(jnp.bfloat16), BLOCK, axis=2)[:, :, None, :]
        if cols == 4 and rows % 2 == 0 and (len(blocks) * BLOCK) % (2 * chips * 8) == 0:
            return fused(weights, keep, sketch, cols, chips, total_rows)
        sampled = jnp.stack(
            [
                lax.psum_scatter(
                    sample(weights, keep, sketch, layer), "col", scatter_dimension=0, tiled=True
                )
                for layer in range(LAYERS)
            ]
        )
        g = [local_gram(sampled[layer]) for layer in range(LAYERS)]
        packed = jnp.stack(
            [
                jnp.concatenate(
                    [
                        x[i * BLOCK : (i + 1) * BLOCK, j * BLOCK : (j + 1) * BLOCK]
                        for i, j in blocks
                    ]
                )
                for x in g
            ]
        )
        gram = lax.psum(packed, ("row", "col"))
        upper = invert(gram, width, total_rows)
        return apply(sampled, upper)

    return body


def solution(mesh):
    return jax.shard_map(
        make_body(mesh),
        mesh=mesh,
        in_specs=(P(None, "row", "col"), P(None, "row", "col"), P("col", None)),
        out_specs=P(None, ("row", "col"), None),
        check_vma=False,
    )
```
